32 devices in a mesh: samp: 8 (over y, x, core), var: 4 (over z).
Axes of the slice: x: 2, y: 2, z: 4, core: 2. Of those that a mesh axis runs over, the one named last changes fastest.
Arguments:
- dosage: bfloat16 [5376, 8192], P('samp', 'var'), may hold values from 0 to 2
- cohort: int32 [5376], P('samp'), may hold values from 0 to 7, as said below
- live_blocks: int32 [8], P('samp'), may hold values from 1 to 7, as said below
- weight_counts: int32 [8], replicated, may hold values from 50 to 1999
Outputs:
- ld_matrix: float32 [8192, 8192], P('samp', 'var')
The draws below stay inside these ranges and needn't reach their ends.
Inputs may be any that keep to these rules, and one draw needn't show every extreme that they name: Every cohort has a live sample on every sample-axis device. live_blocks[i] + live_blocks[i + N/2] = 8 for every i below N/2, N the length of live_blocks; some device has 7.
All inputs are finite; a program needn't handle non-finite values.
Results may differ from the reference program's by a relative error of at most 0.0032.
Values may be sent and summed in bfloat16 or wider, within the bound.
No kernel may reach another device: no remote copies, remote signals or barrier semaphores. Data moves between devices by JAX's collectives and lax.ppermute only.
A program may use at most 128 MiB of HBM per device.

```python
import jax
import jax.numpy as jnp
from jax import lax

V = 8192
COHORTS = 8
BLOCK = 96
HALF = 4
CAP = 7
SAMPLES = 5376
N_SAMP = 8


def cohort_labels(key):
    base = jax.random.fold_in(key, 71)
    drawn = jax.random.randint(base, (SAMPLES,), 0, COHORTS)
    position = jnp.arange(SAMPLES, dtype=jnp.int32) % (CAP * BLOCK)
    return jnp.where(position < COHORTS, position, drawn).astype(jnp.int32)


def draw_cohort(key, part):
    return cohort_labels(key)


def draw_dosage(key, part):
    labels = cohort_labels(key)
    keys = jax.random.split(jax.random.fold_in(key, 5), 4)
    noise = jax.random.normal(keys[0], (SAMPLES, V), jnp.float32)
    lag_one = jax.random.uniform(keys[1], (COHORTS, V), jnp.float32, -0.9, 0.9)
    lag_two = jax.random.uniform(keys[2], (COHORTS, V), jnp.float32, -0.5, 0.5)
    offsets = jax.random.uniform(keys[3], (COHORTS, V), jnp.float32, -1.5, 1.5)
    zero_col = jnp.zeros((SAMPLES, 1), jnp.float32)
    shift_one = jnp.concatenate([zero_col, noise[:, :-1]], axis=1)
    shift_two = jnp.concatenate([zero_col, shift_one[:, :-1]], axis=1)
    latent = noise + lag_one[labels] * shift_one + lag_two[labels] * shift_two
    dosage = 2.0 * jax.nn.sigmoid(0.9 * latent + offsets[labels])
    return dosage.astype(jnp.bfloat16)


def draw_live_blocks(key, part):
    keys = jax.random.split(jax.random.fold_in(key, 13), 3)
    pair_count = N_SAMP // 2
    lower = jax.random.randint(keys[0], (pair_count,), 1, 2 * HALF)
    chosen = jax.random.randint(keys[1], (), 0, pair_count)
    lower = jnp.where(jnp.arange(pair_count) == chosen, CAP, lower)
    flipped = jax.random.randint(keys[2], (pair_count,), 0, 2)
    first_half = jnp.where(flipped == 1, lower, 2 * HALF - lower)
    return jnp.concatenate([first_half, 2 * HALF - first_half]).astype(jnp.int32)


def set_ends(entries, rng, low, largest):
    longest = entries.shape.index(max(entries.shape))
    spots = []
    for shift in (0, 1):
        where = [jax.random.randint(jax.random.fold_in(rng, axis), (), 0, length) for axis, length in enumerate(entries.shape)]
        where[longest] = (where[longest] + shift) % entries.shape[longest]
        spots.append(tuple(where))
    return entries.at[spots[0]].set(low).at[spots[1]].set(largest)


def setup_inputs(seed: int = 0) -> dict:
    key_of = jax.random.split(jax.random.key(seed), 5)
    dosage = draw_dosage(jax.random.fold_in(key_of[4], 71), 0)
    cohort = draw_cohort(jax.random.fold_in(key_of[4], 71), 0)
    live_blocks = draw_live_blocks(jax.random.fold_in(key_of[4], 71), 0)
    weight_counts = set_ends(jax.random.randint(key_of[3], (COHORTS,), 50, 2000), jax.random.fold_in(key_of[3], 1), 50, 1999).astype(jnp.int32)
    return dict(dosage=dosage, cohort=cohort, live_blocks=live_blocks, weight_counts=weight_counts)


EPSILON = 1e-05

def reference(dosage, cohort, live_blocks, weight_counts):
    slot_count = CAP * BLOCK
    position = jnp.arange(SAMPLES, dtype=jnp.int32)
    owner_live = jnp.repeat(live_blocks, slot_count, total_repeat_length=SAMPLES)
    live_mask = (position % slot_count // BLOCK < owner_live).astype(jnp.float32)
    cohort_codes = jnp.arange(COHORTS, dtype=jnp.int32)
    member = jnp.where(cohort[None, :] == cohort_codes[:, None], live_mask[None, :], 0.0).astype(jnp.float32)
    values = dosage.astype(jnp.float32)
    sum_one = jnp.dot(member, values, precision=lax.Precision.HIGHEST)
    sum_two = jnp.dot(member, values * values, precision=lax.Precision.HIGHEST)
    cohort_size = lax.optimization_barrier(jnp.sum(member, axis=1))
    cohort_mean = sum_one / cohort_size[:, None]
    cohort_var = sum_two / cohort_size[:, None] - cohort_mean * cohort_mean
    inv_spread = lax.rsqrt(cohort_var + EPSILON)
    counts_float = weight_counts.astype(jnp.float32)
    cohort_share = counts_float / jnp.sum(counts_float)
    cohort_scale = jnp.sqrt(cohort_share / cohort_size)
    multiplier = inv_spread * cohort_scale[:, None]
    centered = values - cohort_mean[cohort]
    scaled = (live_mask[:, None] * centered * multiplier[cohort]).astype(jnp.bfloat16)
    grouped = scaled.reshape(N_SAMP, slot_count, V)

    def add_group(total, rows):
        partial_value = jnp.dot(rows.T, rows, preferred_element_type=jnp.float32)
        return (total + partial_value, None)
    result, unused = lax.scan(add_group, jnp.zeros((V, V), jnp.float32), grouped)
    return result
```

```python
import functools

import jax
import jax.numpy as jnp
from jax import lax
from jax.experimental import pallas as pl
from jax.experimental.pallas import tpu as pltpu
from jax.sharding import PartitionSpec as P

COHORTS = 8
BLOCK = 96
HALF = 4
EPSILON = 1e-05
PARTS = 3
TABLE = 128


def swapped(block, distance):
    return lax.ppermute(
        block, "samp", [(i, i ^ distance) for i in range(lax.axis_size("samp"))]
    )


def route(start, count):
    down, up = list(range(start - 1, -1, -1)), list(range(start + 1, count))
    return [start] + (down + up if start < count // 2 else up + down)


def split_parts(table):
    parts, rest = [], table
    for _ in range(PARTS):
        part = lax.reduce_precision(rest, exponent_bits=8, mantissa_bits=7)
        parts.append(part.astype(jnp.bfloat16))
        rest = rest - part
    used = PARTS * COHORTS
    parts.append(jnp.zeros((TABLE - used, table.shape[1]), jnp.bfloat16))
    return jnp.concatenate(parts, 0)


def sums_kernel(member_ref, dose_ref, sums_ref):
    member = member_ref[...]
    dose = dose_ref[...]
    wide = dose.astype(jnp.float32)
    square = wide * wide
    high = square.astype(jnp.bfloat16)
    low = (square - high.astype(jnp.float32)).astype(jnp.bfloat16)
    dot = functools.partial(jnp.dot, preferred_element_type=jnp.float32)
    sums_ref[:COHORTS, :] = dot(member, dose)[:COHORTS]
    sums_ref[COHORTS:, :] = (dot(member, high) + dot(member, low))[:COHORTS]


def cohort_sums(member, dose):
    rows, columns = dose.shape
    tile = min(512, columns)
    return pl.pallas_call(
        sums_kernel,
        grid=(columns // tile,),
        in_specs=[
            pl.BlockSpec((16, rows), lambda j: (0, 0)),
            pl.BlockSpec((rows, tile), lambda j: (0, j)),
        ],
        out_specs=pl.BlockSpec((2 * COHORTS, tile), lambda j: (0, j)),
        out_shape=jax.ShapeDtypeStruct((2 * COHORTS, columns), jnp.float32),
        cost_estimate=pl.CostEstimate(
            flops=6 * 16 * rows * columns, bytes_accessed=2 * rows * columns, transcendentals=0
        ),
        compiler_params=pltpu.CompilerParams(vmem_limit_bytes=24 * 2**20),
    )(member, dose)


def standardized(dose, onehot, mean_table, scale_table):
    dot = functools.partial(jnp.dot, preferred_element_type=jnp.float32)
    centered = dose.astype(jnp.float32) - dot(onehot, mean_table)
    return (centered * dot(onehot, scale_table)).astype(jnp.bfloat16)


def gram_kernel(sizes, has_total, *refs):
    n = len(sizes)
    cols, rows, hots = refs[:n], refs[n : 2 * n], refs[2 * n : 3 * n]
    col_mean, col_scale, row_mean, row_scale = refs[3 * n : 3 * n + 4]
    rest = refs[3 * n + 4 :]
    out, row_ready, col_ready = rest[-3:]

    @pl.when(pl.program_id(0) == 0)
    def _():
        at = 0
        for j, size in enumerate(sizes):
            ready = standardized(rows[j][...], hots[j][...], row_mean[...], row_scale[...])
            row_ready[:, at : at + size] = ready.T
            at += size

    at = 0
    for j, size in enumerate(sizes):
        col_ready[at : at + size, :] = standardized(
            cols[j][...], hots[j][...], col_mean[...], col_scale[...]
        )
        at += size
    product = jnp.dot(row_ready[...], col_ready[...], preferred_element_type=jnp.float32)
    if has_total:
        product += rest[0][...]
    out[...] = product


def gram(total, cols, rows, hots, col_tables, row_tables):
    sizes = tuple(c.shape[0] for c in cols)
    depth, width, height = sum(sizes), cols[0].shape[1], rows[0].shape[1]
    tile = min(512, width)
    whole = lambda shape: pl.BlockSpec(shape, lambda j: (0, 0))
    by_tile = lambda height: pl.BlockSpec((height, tile), lambda j: (0, j))
    in_specs = (
        [by_tile(s) for s in sizes]
        + [whole((s, height)) for s in sizes]
        + [whole((s, TABLE)) for s in sizes]
        + [by_tile(TABLE)] * 2
        + [whole((TABLE, height))] * 2
    )
    operands = [*cols, *rows, *hots, *col_tables, *row_tables]
    aliases = {}
    if total is not None:
        aliases = {len(operands): 0}
        operands.append(total)
        in_specs.append(by_tile(height))
    return pl.pallas_call(
        functools.partial(gram_kernel, sizes, total is not None),
        grid=(width // tile,),
        in_specs=in_specs,
        out_specs=by_tile(height),
        out_shape=jax.ShapeDtypeStruct((height, width), jnp.float32),
        scratch_shapes=[
            pltpu.VMEM((height, depth), jnp.bfloat16),
            pltpu.VMEM((depth, tile), jnp.bfloat16),
        ],
        input_output_aliases=aliases,
        cost_estimate=pl.CostEstimate(
            flops=2 * depth * height * width,
            bytes_accessed=8 * height * width + 2 * depth * (height + width),
            transcendentals=0,
        ),
        compiler_params=pltpu.CompilerParams(vmem_limit_bytes=48 * 2**20),
    )(*operands)


def shards(dosage, cohort, live_blocks, weight_counts):
    n_samp, n_var = lax.axis_size("samp"), lax.axis_size("var")
    samp, var = lax.axis_index("samp"), lax.axis_index("var")
    slots, width = dosage.shape
    height = width * n_var // n_samp
    kept = HALF * BLOCK
    owner = [i * height // width for i in range(n_samp)]
    routes = [route(owner[i], n_var) for i in range(n_samp)]
    place_on_route = [[r.index(v) for v in range(n_var)] for r in routes]
    place = jnp.asarray(place_on_route, jnp.int32)[samp, var]
    row_start = samp * height % width
    bits = [n_samp >> (b + 1) for b in range(n_samp.bit_length() - 1)]

    def along_line(block):
        result = moving = block
        for hop in range(1, n_var):
            pairs = [
                (s * n_var + r[hop - 1], s * n_var + r[hop]) for s, r in enumerate(routes)
            ]
            moving = lax.ppermute(moving, ("samp", "var"), pairs)
            result = jnp.where(place == hop, moving, result)
        return result

    def row_part(block):
        return lax.dynamic_slice_in_dim(block, row_start, height, 1)

    own_live = live_blocks[0]
    info = jnp.concatenate([cohort, jnp.broadcast_to(own_live, (TABLE,))])
    infos = lax.all_gather(info, "samp", axis=0)
    surplus = swapped(dosage[kept:], n_samp // 2)

    position = lax.broadcasted_iota(jnp.int32, (16, slots), 1)
    label = lax.broadcasted_iota(jnp.int32, (16, slots), 0)
    member = (cohort[None, :] == label) & (position < own_live * BLOCK)
    sums = cohort_sums(member.astype(jnp.bfloat16), dosage)
    for bit in bits:
        sums = sums + swapped(sums, bit)

    offset = own_live * BLOCK
    placed = lax.dynamic_update_slice_in_dim(jnp.zeros_like(dosage), surplus, offset, 0)
    row_index = lax.broadcasted_iota(jnp.int32, (kept, 1), 0)
    balanced = jnp.where(row_index < offset, dosage[:kept], placed[:kept])

    pieces = [(0, balanced)]
    for bit in bits:
        pieces += [(m ^ bit, swapped(block, bit)) for m, block in pieces]
    order = [m for m, _ in pieces]

    lives = infos[:, slots]
    codes = infos[:, :slots]
    devices = jnp.arange(n_samp)
    partner = codes[devices ^ (n_samp // 2)]
    slot = lax.broadcasted_iota(jnp.int32, (n_samp, kept), 1)
    moved_from = kept + slot - lives[:, None] * BLOCK
    moved = jnp.take_along_axis(partner, jnp.clip(moved_from, 0, slots - 1), axis=1)
    codes = jnp.where(slot < lives[:, None] * BLOCK, codes[:, :kept], moved)
    cohort_size = jnp.sum(
        (codes[None] == jnp.arange(COHORTS)[:, None, None]).astype(jnp.float32), axis=(1, 2)
    )
    lane = lax.broadcasted_iota(jnp.int32, (kept, TABLE), 1)
    lane = jnp.where(lane < PARTS * COHORTS, lane % COHORTS, -1)
    hots = [
        (codes[samp ^ m][:, None] == lane).astype(jnp.bfloat16) for m in order
    ]

    sum_one, sum_two = sums[:COHORTS], sums[COHORTS:]
    cohort_mean = sum_one / cohort_size[:, None]
    cohort_var = sum_two / cohort_size[:, None] - cohort_mean * cohort_mean
    inv_spread = lax.rsqrt(cohort_var + EPSILON)
    counts_float = weight_counts.astype(jnp.float32)
    cohort_share = counts_float / jnp.sum(counts_float)
    multiplier = inv_spread * jnp.sqrt(cohort_share / cohort_size)[:, None]
    tables = jnp.concatenate([cohort_mean, multiplier], 0)
    row_tables = along_line(row_part(tables))
    col_tables = [split_parts(cohort_mean), split_parts(multiplier)]
    row_tables = [split_parts(row_tables[:COHORTS]), split_parts(row_tables[COHORTS:])]

    rows = [along_line(row_part(block)) for _, block in pieces]
    cols = [block for _, block in pieces]
    total = None
    step = max(1, len(cols) // 4)
    for at in range(0, len(cols), step):
        part = slice(at, at + step)
        total = gram(total, cols[part], rows[part], hots[part], col_tables, row_tables)
    return total


def solution(mesh):
    placed = (P("samp", "var"), P("samp"), P("samp"), P())
    return jax.shard_map(
        shards, mesh=mesh, in_specs=placed, out_specs=P("samp", "var"), check_vma=False
    )
```

```python
import functools

import jax
import jax.numpy as jnp
from jax import lax
from jax.experimental import pallas as pl
from jax.experimental.pallas import tpu as pltpu
from jax.sharding import PartitionSpec as P

COHORTS = 8
BLOCK = 96
HALF = 4
EPSILON = 1e-05
PARTS = 3
TABLE = 128


def swapped(block, distance):
    return lax.ppermute(
        block, "samp", [(i, i ^ distance) for i in range(lax.axis_size("samp"))]
    )


def hops(owner, count):
    if count == 4:
        low = owner < 2
        middle = 2 if low else 1
        ends = [p for p in range(4) if p not in (owner, middle)]
        ends.sort(reverse=low)
        return [(0, owner, middle)] + [(i + 1, middle, e) for i, e in enumerate(ends)]
    down, up = list(range(owner - 1, -1, -1)), list(range(owner + 1, count))
    visited = [owner] + (down + up if owner < count // 2 else up + down)
    return [(i, visited[i], visited[i + 1]) for i in range(count - 1)]


def split_parts(table):
    parts, rest = [], table
    for _ in range(PARTS):
        part = lax.reduce_precision(rest, exponent_bits=8, mantissa_bits=7)
        parts.append(part.astype(jnp.bfloat16))
        rest = rest - part
    used = PARTS * COHORTS
    parts.append(jnp.zeros((TABLE - used, table.shape[1]), jnp.bfloat16))
    return jnp.concatenate(parts, 0)


def sums_kernel(member_ref, dose_ref, sums_ref):
    member = member_ref[...]
    dose = dose_ref[...]
    wide = dose.astype(jnp.float32)
    square = wide * wide
    high = square.astype(jnp.bfloat16)
    low = (square - high.astype(jnp.float32)).astype(jnp.bfloat16)
    dot = functools.partial(jnp.dot, preferred_element_type=jnp.float32)
    sums_ref[:COHORTS, :] = dot(member, dose)[:COHORTS]
    sums_ref[COHORTS:, :] = (dot(member, high) + dot(member, low))[:COHORTS]


def cohort_sums(member, dose):
    rows, columns = dose.shape
    tile = min(512, columns)
    return pl.pallas_call(
        sums_kernel,
        grid=(columns // tile,),
        in_specs=[
            pl.BlockSpec((16, rows), lambda j: (0, 0)),
            pl.BlockSpec((rows, tile), lambda j: (0, j)),
        ],
        out_specs=pl.BlockSpec((2 * COHORTS, tile), lambda j: (0, j)),
        out_shape=jax.ShapeDtypeStruct((2 * COHORTS, columns), jnp.float32),
        cost_estimate=pl.CostEstimate(
            flops=6 * 16 * rows * columns, bytes_accessed=2 * rows * columns, transcendentals=0
        ),
        compiler_params=pltpu.CompilerParams(vmem_limit_bytes=24 * 2**20),
    )(member, dose)


def standardize_kernel(dose_ref, code_ref, mean_ref, scale_ref, out_ref):
    code = code_ref[...].astype(jnp.float32)
    lane = lax.broadcasted_iota(jnp.int32, code.shape, 1)
    cohort = jnp.where(lane < PARTS * COHORTS, lane % COHORTS, -1)
    hot = (code == cohort.astype(jnp.float32)).astype(jnp.float32).astype(jnp.bfloat16)
    dot = functools.partial(jnp.dot, preferred_element_type=jnp.float32)
    centered = dose_ref[...].astype(jnp.float32) - dot(hot, mean_ref[...])
    out_ref[...] = (centered * dot(hot, scale_ref[...])).astype(jnp.bfloat16)


def standardized(coded, tables):
    rows, width = coded.shape[0], coded.shape[1] - TABLE
    tile = min(512, width)
    by_tile = lambda height: pl.BlockSpec((height, tile), lambda j: (0, j))
    return pl.pallas_call(
        standardize_kernel,
        grid=(width // tile,),
        in_specs=[
            by_tile(rows),
            pl.BlockSpec((rows, TABLE), lambda j: (0, width // TABLE)),
            by_tile(TABLE),
            by_tile(TABLE),
        ],
        out_specs=by_tile(rows),
        out_shape=jax.ShapeDtypeStruct((rows, width), jnp.bfloat16),
        cost_estimate=pl.CostEstimate(
            flops=4 * TABLE * rows * width, bytes_accessed=4 * rows * width, transcendentals=0
        ),
        compiler_params=pltpu.CompilerParams(vmem_limit_bytes=24 * 2**20),
    )(coded, coded, *tables)


def gram_kernel(takes, row_sizes, row_counts, has_total, *refs):
    n = len(takes)
    role, cols, refs = refs[0][0], refs[1 : n + 1], refs[n + 1 :]
    rows = []
    for count in row_counts:
        rows.append(refs[:count])
        refs = refs[count:]
    total = refs[0] if has_total else None
    out, row_dose, row_ready, col_ready, sems = refs[-5:]
    depth = sum(row_sizes)

    @pl.when(pl.program_id(0) == 0)
    def _():
        at, waits = 0, []
        for j, (places, size) in enumerate(zip(rows, row_sizes)):
            to = row_dose.at[pl.ds(at, size), :]
            for i, place in enumerate(places):
                here = role == i if i < len(places) - 1 else role >= i

                @pl.when(here)
                def _():
                    pltpu.make_async_copy(place, to, sems.at[j]).start()

            waits.append(pltpu.make_async_copy(places[0], to, sems.at[j]))
            at += size
        for wait in waits:
            wait.wait()
        step = 128 if depth % 128 == 0 else depth
        for at in range(0, depth, step):
            row_ready[:, at : at + step] = row_dose[at : at + step, :].T

    at = 0
    for j, (start, size) in enumerate(takes):
        col_ready[at : at + size, :] = cols[j][start : start + size, :]
        at += size
    product = jnp.dot(row_ready[...], col_ready[...], preferred_element_type=jnp.float32)
    if has_total:
        product += total[...]
    out[...] = product


def gram(total, role, cols, rows):
    takes = tuple((start, size) for _, start, size in cols)
    blocks = [block for block, _, _ in cols]
    row_sizes = tuple(r[0].shape[0] for r in rows)
    depth, width, height = sum(row_sizes), blocks[0].shape[1], rows[0][0].shape[1]
    tile = min(512, width)
    by_tile = lambda height: pl.BlockSpec((height, tile), lambda j: (0, j))
    in_specs = (
        [pl.BlockSpec(memory_space=pltpu.SMEM)]
        + [by_tile(start + size) for start, size in takes]
        + [pl.BlockSpec(memory_space=pl.ANY) for r in rows for _ in r]
    )
    operands = [role, *blocks, *(part for r in rows for part in r)]
    aliases = {}
    if total is not None:
        aliases = {len(operands): 0}
        operands.append(total)
        in_specs.append(by_tile(height))
    return pl.pallas_call(
        functools.partial(
            gram_kernel, takes, row_sizes, tuple(len(r) for r in rows), total is not None
        ),
        grid=(width // tile,),
        in_specs=in_specs,
        out_specs=by_tile(height),
        out_shape=jax.ShapeDtypeStruct((height, width), jnp.float32),
        scratch_shapes=[
            pltpu.VMEM((depth, height), jnp.bfloat16),
            pltpu.VMEM((height, depth), jnp.bfloat16),
            pltpu.VMEM((depth, tile), jnp.bfloat16),
            pltpu.SemaphoreType.DMA((len(rows),)),
        ],
        input_output_aliases=aliases,
        cost_estimate=pl.CostEstimate(
            flops=2 * depth * height * width,
            bytes_accessed=8 * height * width + 2 * depth * (height + width),
            transcendentals=0,
        ),
        compiler_params=pltpu.CompilerParams(vmem_limit_bytes=48 * 2**20),
    )(*operands)


def gram_of(groups, role, at_once):
    total = None
    for at in range(0, len(groups), at_once):
        part = groups[at : at + at_once]
        cols = [c for g in part for c in g[0]]
        total = gram(total, role, cols, [r for g in part for r in g[1]])
    return total


def after(block, *done):
    return lax.optimization_barrier((block, *done))[0]


def shards(dosage, cohort, live_blocks, weight_counts):
    n_samp, n_var = lax.axis_size("samp"), lax.axis_size("var")
    samp, var = lax.axis_index("samp"), lax.axis_index("var")
    slots, width = dosage.shape
    height = width * n_var // n_samp
    kept = HALF * BLOCK
    owner = [i * height // width for i in range(n_samp)]
    owns_rows = samp * height // width == var
    lines = [hops(o, n_var) for o in owner]
    reached = [[0] * n_var for _ in range(n_samp)]
    for s, line in enumerate(lines):
        for step, _, end in line:
            reached[s][end] = step + 1
    here = (jnp.arange(n_samp)[:, None] == samp) & (jnp.arange(n_var)[None, :] == var)
    role = jnp.sum(jnp.where(here, jnp.asarray(reached, jnp.int32), 0)).reshape(1)
    row_start = samp * height % width
    early = BLOCK if (n_samp, n_var) == (8, 4) else 0
    bits = [n_samp >> (b + 1) for b in range(n_samp.bit_length() - 1)]
    def hop(block, step):
        pairs = [
            (s * n_var + line[step][1], s * n_var + line[step][2]) for s, line in enumerate(lines)
        ]
        return lax.ppermute(block, ("samp", "var"), pairs)

    def along_line(block, *done):
        got = []
        for step in range(n_var - 1):
            source = [k for k in range(step) if lines[0][k][2] == lines[0][step][1]]
            moving = got[source[0]] if source else block
            got.append(hop(after(moving, *done) if source and done else moving, step))
        return [block, *got]

    def along_var(block, shift):
        pairs = [(v, v + shift) for v in range(n_var) if 0 <= v + shift < n_var]
        return lax.ppermute(block, "var", pairs)

    def row_part(block, start, size):
        return lax.dynamic_slice(block, (start, row_start), (size, height))

    own_live = live_blocks[0]
    code = cohort.astype(jnp.bfloat16)
    coded = jnp.concatenate([dosage, jnp.broadcast_to(code[:, None], (slots, TABLE))], 1)

    position = lax.broadcasted_iota(jnp.int32, (16, slots), 1)
    label = lax.broadcasted_iota(jnp.int32, (16, slots), 0)
    member = (cohort[None, :] == label) & (position < own_live * BLOCK)
    counts = jnp.sum(member.astype(jnp.float32), axis=1, keepdims=True)
    sums = cohort_sums(member.astype(jnp.bfloat16), dosage)
    extra = [jnp.broadcast_to(counts, (2 * COHORTS, TABLE))]
    if early:
        row = lax.broadcasted_iota(jnp.int32, (2 * COHORTS, early), 0)
        slot_codes = jnp.where(row == samp, cohort[None, :early].astype(jnp.float32), 0.0)
        extra.append(jnp.pad(slot_codes, ((0, 0), (0, TABLE - early))))
    sums = jnp.concatenate([sums, *extra], 1)
    surplus = swapped(coded[kept:], bits[0])
    for bit in bits[1:]:
        sums = sums + swapped(sums, bit)
    sums = sums + swapped(after(sums, surplus), bits[0])
    below, above = [dosage[:early]], [dosage[:early]]
    if early:
        for _ in range(n_var - 1):
            below.append(along_var(below[-1], 1))
            above.append(along_var(above[-1], -1))

    sum_one, sum_two = sums[:COHORTS, :width], sums[COHORTS:, :width]
    cohort_size = sums[:COHORTS, width]
    cohort_mean = sum_one / cohort_size[:, None]
    cohort_var = sum_two / cohort_size[:, None] - cohort_mean * cohort_mean
    inv_spread = lax.rsqrt(cohort_var + EPSILON)
    counts_float = weight_counts.astype(jnp.float32)
    cohort_share = counts_float / jnp.sum(counts_float)
    multiplier = inv_spread * jnp.sqrt(cohort_share / cohort_size)[:, None]
    tables = [split_parts(cohort_mean), split_parts(multiplier)]

    offset = own_live * BLOCK
    placed = lax.dynamic_update_slice_in_dim(jnp.zeros_like(coded), surplus, offset, 0)
    row_index = lax.broadcasted_iota(jnp.int32, (kept, 1), 0)
    balanced = jnp.where(row_index < offset, coded[:kept], placed[:kept])
    if early:
        balanced = after(balanced, below[2], above[2])
    base = standardized(balanced, tables)
    if not early:
        pieces = {0: base}
        for bit in bits:
            pieces |= {m ^ bit: swapped(block, bit) for m, block in pieces.items()}
        groups = []
        for m in range(0, n_samp, 2):
            cols = [(pieces[i], 0, kept) for i in (m, m + 1)]
            rows = along_line(jnp.concatenate([row_part(p, 0, kept) for p, _, _ in cols], 0))
            if n_var > 4:
                rows = [rows[0], sum(rows[2:], rows[1])]
            groups.append((cols, [rows]))
        return gram_of(groups, role, 3)

    def of_panel(panel):
        chosen = jnp.zeros_like(below[0])
        for h in range(1, n_var):
            chosen += jnp.where(panel == var - h, below[h], jnp.zeros_like(below[h]))
            chosen += jnp.where(panel == var + h, above[h], jnp.zeros_like(above[h]))
        return chosen

    chip = samp // 2
    far, near, both = 4, 2, 6
    size, used = kept - early, PARTS * COHORTS
    rest = lambda m: pieces[m][early:]
    panel = lambda got: jnp.where(owns_rows, got[0], sum(got[2:], got[1]))
    other_half = lambda block: lax.dynamic_slice_in_dim(block, height - row_start, height, 1)
    my_half = lambda block: row_part(block, 0, block.shape[0])

    pieces = {0: base}
    pieces[far], pieces[near] = swapped(base, far), swapped(base, near)
    first = jnp.concatenate([rest(0), *(t[:used] for t in tables)], 0)
    legs = [along_line(first)]
    pieces[1] = swapped(base, 1)
    legs.append(along_line(after(rest(near), pieces[1], below[3], above[3])))
    pieces[both] = swapped(after(pieces[far], pieces[near], legs[0][1]), near)
    legs.append(along_line(after(rest(far), legs[0][1])))
    up = jnp.concatenate([of_panel(chip ^ 2), of_panel(chip ^ 3)], 0)
    up = swapped(after(up, legs[1][1]), far)
    pieces[both + 1] = swapped(after(pieces[both], *legs[0][2:], legs[1][1]), 1)
    done = (legs[2][1], *legs[1][2:])
    tail = [row_part(pieces[m], early, size) for m in (both, both + 1)]
    legs.append(along_line(after(tail[0], *done), *legs[2][2:]))
    legs.append(along_line(after(tail[1], *done), *legs[2][2:], *legs[3][2:]))
    aside = jnp.concatenate([of_panel(chip ^ 1), up[early:]], 0)
    aside = swapped(after(aside, *done), near)
    brought = jnp.concatenate([of_panel(chip), aside[:early], up[:early], aside[early:]], 0)
    other = swapped(brought, 1)
    pieces[far + 1] = swapped(after(pieces[far], pieces[both + 1]), 1)
    pieces[near + 1] = swapped(after(pieces[near], pieces[far + 1]), 1)
    whole = [panel([part[:size] for part in leg]) for leg in legs[:3]]
    others = [swapped(other_half(block), 1) for block in whole]

    row_tables = my_half(panel([part[size:] for part in legs[0]]))
    pad = jnp.zeros((TABLE - used, height), jnp.bfloat16)
    row_tables = [jnp.concatenate([row_tables[i : i + used], pad], 0) for i in (0, used)]
    order = [*range(0, n_samp, 2), *range(1, n_samp, 2)]
    source = samp ^ jnp.asarray(order, jnp.int32)
    pick = (source[:, None] == jnp.arange(n_samp)[None, :]).astype(jnp.float32)
    early_codes = jnp.dot(pick, sums[:n_samp, width + TABLE : width + TABLE + early])
    lanes = jnp.broadcast_to(early_codes.reshape(-1, 1), (n_samp * early, TABLE))
    brought = jnp.concatenate([my_half(brought), my_half(other)], 0)
    brought = standardized(jnp.concatenate([brought, lanes.astype(jnp.bfloat16)], 1), row_tables)
    own = jnp.concatenate([row_part(pieces[m], 0, early) for m in order], 0)

    cols = lambda *ms: [(pieces[m], early, size) for m in ms]
    groups = [([(pieces[m], 0, early) for m in order], [[own, brought]])]
    groups += [
        (cols(i, i + 1), [[my_half(block)], [other]])
        for i, block, other in zip((0, near, far), whole, others)
    ]
    groups.append((cols(both, both + 1), legs[3:]))
    return gram_of(groups, role, 3)


def solution(mesh):
    placed = (P("samp", "var"), P("samp"), P("samp"), P())
    return jax.shard_map(
        shards, mesh=mesh, in_specs=placed, out_specs=P("samp", "var"), check_vma=False
    )
```

```python
import functools

import jax
import jax.numpy as jnp
from jax import lax
from jax.experimental import pallas as pl
from jax.experimental.pallas import tpu as pltpu
from jax.sharding import PartitionSpec as P

COHORTS = 8
BLOCK = 96
HALF = 4
EPSILON = 1e-05
PARTS = 3
TABLE = 128


def swapped(block, distance):
    return lax.ppermute(
        block, "samp", [(i, i ^ distance) for i in range(lax.axis_size("samp"))]
    )


def hops(owner, count):
    if count == 4:
        low = owner < 2
        middle = 2 if low else 1
        ends = [p for p in range(4) if p not in (owner, middle)]
        ends.sort(reverse=low)
        return [(0, owner, middle)] + [(i + 1, middle, e) for i, e in enumerate(ends)]
    down, up = list(range(owner - 1, -1, -1)), list(range(owner + 1, count))
    visited = [owner] + (down + up if owner < count // 2 else up + down)
    return [(i, visited[i], visited[i + 1]) for i in range(count - 1)]


def split_parts(table):
    parts, rest = [], table
    for _ in range(PARTS):
        part = lax.reduce_precision(rest, exponent_bits=8, mantissa_bits=7)
        parts.append(part.astype(jnp.bfloat16))
        rest = rest - part
    used = PARTS * COHORTS
    parts.append(jnp.zeros((TABLE - used, table.shape[1]), jnp.bfloat16))
    return jnp.concatenate(parts, 0)


def sums_kernel(member_ref, dose_ref, sums_ref):
    member = member_ref[...]
    dose = dose_ref[...]
    wide = dose.astype(jnp.float32)
    square = wide * wide
    high = square.astype(jnp.bfloat16)
    low = (square - high.astype(jnp.float32)).astype(jnp.bfloat16)
    dot = functools.partial(jnp.dot, preferred_element_type=jnp.float32)
    sums_ref[:COHORTS, :] = dot(member, dose)[:COHORTS]
    sums_ref[COHORTS:, :] = (dot(member, high) + dot(member, low))[:COHORTS]


def cohort_sums(member, dose):
    rows, columns = dose.shape
    tile = min(512, columns)
    return pl.pallas_call(
        sums_kernel,
        grid=(columns // tile,),
        in_specs=[
            pl.BlockSpec((16, rows), lambda j: (0, 0)),
            pl.BlockSpec((rows, tile), lambda j: (0, j)),
        ],
        out_specs=pl.BlockSpec((2 * COHORTS, tile), lambda j: (0, j)),
        out_shape=jax.ShapeDtypeStruct((2 * COHORTS, columns), jnp.float32),
        cost_estimate=pl.CostEstimate(
            flops=6 * 16 * rows * columns, bytes_accessed=2 * rows * columns, transcendentals=0
        ),
        compiler_params=pltpu.CompilerParams(vmem_limit_bytes=24 * 2**20),
    )(member, dose)


def standardize_kernel(skip, dose_ref, code_ref, mean_ref, scale_ref, *refs):
    code = code_ref[...].astype(jnp.float32)
    lane = lax.broadcasted_iota(jnp.int32, code.shape, 1)
    cohort = jnp.where(lane < PARTS * COHORTS, lane % COHORTS, -1)
    hot = (code == cohort.astype(jnp.float32)).astype(jnp.float32).astype(jnp.bfloat16)
    dot = functools.partial(jnp.dot, preferred_element_type=jnp.float32)
    centered = dose_ref[...].astype(jnp.float32) - dot(hot, mean_ref[...])
    ready = (centered * dot(hot, scale_ref[...])).astype(jnp.bfloat16)
    if len(refs) == 1:
        refs[0][...] = ready
    else:
        extra_ref, out_ref, rest_ref = refs
        kept = ready.shape[0] - skip
        out_ref[...] = ready
        rest_ref[:kept, :] = ready[skip:]
        rest_ref[kept:, :] = extra_ref[...]


def standardized(coded, tables, extra=None, skip=0):
    rows, width = coded.shape[0], coded.shape[1] - TABLE
    tile = min(512, width)
    by_tile = lambda height: pl.BlockSpec((height, tile), lambda j: (0, j))
    heights = [rows] if extra is None else [rows, rows - skip + extra.shape[0]]
    out = pl.pallas_call(
        functools.partial(standardize_kernel, skip),
        grid=(width // tile,),
        in_specs=[
            by_tile(rows),
            pl.BlockSpec((rows, TABLE), lambda j: (0, width // TABLE)),
            by_tile(TABLE),
            by_tile(TABLE),
        ]
        + ([] if extra is None else [by_tile(extra.shape[0])]),
        out_specs=[by_tile(h) for h in heights],
        out_shape=[jax.ShapeDtypeStruct((h, width), jnp.bfloat16) for h in heights],
        cost_estimate=pl.CostEstimate(
            flops=4 * TABLE * rows * width, bytes_accessed=4 * rows * width, transcendentals=0
        ),
        compiler_params=pltpu.CompilerParams(vmem_limit_bytes=24 * 2**20),
    )(coded, coded, *tables, *([] if extra is None else [extra]))
    return out[0] if extra is None else out


def gram_kernel(takes, row_sizes, row_counts, has_total, *refs):
    n = len(takes)
    role, cols, refs = refs[0][0], refs[1 : n + 1], refs[n + 1 :]
    rows = []
    for count in row_counts:
        rows.append(refs[:count])
        refs = refs[count:]
    total = refs[0] if has_total else None
    out, row_ready, col_ready, sems = refs[-4:]

    @pl.when(pl.program_id(0) == 0)
    def _():
        at, waits = 0, []
        for j, (places, size) in enumerate(zip(rows, row_sizes)):
            to = row_ready.at[pl.ds(at, size), :]
            for i, place in enumerate(places):
                here = role == i if i < len(places) - 1 else role >= i

                @pl.when(here)
                def _():
                    pltpu.make_async_copy(place, to, sems.at[j]).start()

            waits.append(pltpu.make_async_copy(places[0], to, sems.at[j]))
            at += size
        for wait in waits:
            wait.wait()

    at = 0
    for j, (start, size) in enumerate(takes):
        col_ready[at : at + size, :] = cols[j][start : start + size, :]
        at += size
    product = lax.dot_general(
        row_ready[...],
        col_ready[...],
        (((0,), (0,)), ((), ())),
        preferred_element_type=jnp.float32,
    )
    if has_total:
        product += total[...]
    out[...] = product


def gram(total, role, cols, rows):
    takes = tuple((start, size) for _, start, size in cols)
    blocks = [block for block, _, _ in cols]
    row_sizes = tuple(r[0].shape[0] for r in rows)
    depth, width, height = sum(row_sizes), blocks[0].shape[1], rows[0][0].shape[1]
    tile = min(512, width)
    by_tile = lambda height: pl.BlockSpec((height, tile), lambda j: (0, j))
    in_specs = (
        [pl.BlockSpec(memory_space=pltpu.SMEM)]
        + [by_tile(start + size) for start, size in takes]
        + [pl.BlockSpec(memory_space=pl.ANY) for r in rows for _ in r]
    )
    operands = [role, *blocks, *(part for r in rows for part in r)]
    aliases = {}
    if total is not None:
        aliases = {len(operands): 0}
        operands.append(total)
        in_specs.append(by_tile(height))
    return pl.pallas_call(
        functools.partial(
            gram_kernel, takes, row_sizes, tuple(len(r) for r in rows), total is not None
        ),
        grid=(width // tile,),
        in_specs=in_specs,
        out_specs=by_tile(height),
        out_shape=jax.ShapeDtypeStruct((height, width), jnp.float32),
        scratch_shapes=[
            pltpu.VMEM((depth, height), jnp.bfloat16),
            pltpu.VMEM((depth, tile), jnp.bfloat16),
            pltpu.SemaphoreType.DMA((len(rows),)),
        ],
        input_output_aliases=aliases,
        cost_estimate=pl.CostEstimate(
            flops=2 * depth * height * width,
            bytes_accessed=8 * height * width + 2 * depth * (height + width),
            transcendentals=0,
        ),
        compiler_params=pltpu.CompilerParams(vmem_limit_bytes=48 * 2**20),
    )(*operands)


def gram_of(groups, role, at_once):
    total = None
    for at in range(0, len(groups), at_once):
        part = groups[at : at + at_once]
        cols = [c for g in part for c in g[0]]
        total = gram(total, role, cols, [r for g in part for r in g[1]])
    return total


def after(block, *done):
    return lax.optimization_barrier((block, *done))[0]


def shards(dosage, cohort, live_blocks, weight_counts):
    n_samp, n_var = lax.axis_size("samp"), lax.axis_size("var")
    samp, var = lax.axis_index("samp"), lax.axis_index("var")
    slots, width = dosage.shape
    height = width * n_var // n_samp
    kept = HALF * BLOCK
    owner = [i * height // width for i in range(n_samp)]
    owns_rows = samp * height // width == var
    lines = [hops(o, n_var) for o in owner]
    reached = [[0] * n_var for _ in range(n_samp)]
    for s, line in enumerate(lines):
        for step, _, end in line:
            reached[s][end] = step + 1
    here = (jnp.arange(n_samp)[:, None] == samp) & (jnp.arange(n_var)[None, :] == var)
    role = jnp.sum(jnp.where(here, jnp.asarray(reached, jnp.int32), 0)).reshape(1)
    row_start = samp * height % width
    early = BLOCK if (n_samp, n_var) == (8, 4) else 0
    bits = [n_samp >> (b + 1) for b in range(n_samp.bit_length() - 1)]
    def hop(block, step):
        pairs = [
            (s * n_var + line[step][1], s * n_var + line[step][2]) for s, line in enumerate(lines)
        ]
        return lax.ppermute(block, ("samp", "var"), pairs)

    def along_line(block, *done):
        got = []
        for step in range(n_var - 1):
            source = [k for k in range(step) if lines[0][k][2] == lines[0][step][1]]
            moving = got[source[0]] if source else block
            got.append(hop(after(moving, *done) if source and done else moving, step))
        return [block, *got]

    def along_var(block, shift):
        pairs = [(v, v + shift) for v in range(n_var) if 0 <= v + shift < n_var]
        return lax.ppermute(block, "var", pairs)

    def row_part(block, start, size):
        return lax.dynamic_slice(block, (start, row_start), (size, height))

    own_live = live_blocks[0]
    code = cohort.astype(jnp.bfloat16)
    coded = jnp.concatenate([dosage, jnp.broadcast_to(code[:, None], (slots, TABLE))], 1)

    position = lax.broadcasted_iota(jnp.int32, (16, slots), 1)
    label = lax.broadcasted_iota(jnp.int32, (16, slots), 0)
    member = (cohort[None, :] == label) & (position < own_live * BLOCK)
    counts = jnp.sum(member.astype(jnp.float32), axis=1, keepdims=True)
    sums = cohort_sums(member.astype(jnp.bfloat16), dosage)
    extra = [jnp.broadcast_to(counts, (2 * COHORTS, TABLE))]
    if early:
        row = lax.broadcasted_iota(jnp.int32, (2 * COHORTS, early), 0)
        slot_codes = jnp.where(row == samp, cohort[None, :early].astype(jnp.float32), 0.0)
        extra.append(jnp.pad(slot_codes, ((0, 0), (0, TABLE - early))))
    sums = jnp.concatenate([sums, *extra], 1)
    surplus = swapped(coded[kept:], bits[0])
    for bit in bits[1:]:
        sums = sums + swapped(sums, bit)
    sums = sums + swapped(after(sums, surplus), bits[0])
    below, above = [dosage[:early]], [dosage[:early]]
    if early:
        for _ in range(n_var - 1):
            below.append(along_var(below[-1], 1))
            above.append(along_var(above[-1], -1))

    sum_one, sum_two = sums[:COHORTS, :width], sums[COHORTS:, :width]
    cohort_size = sums[:COHORTS, width]
    cohort_mean = sum_one / cohort_size[:, None]
    cohort_var = sum_two / cohort_size[:, None] - cohort_mean * cohort_mean
    inv_spread = lax.rsqrt(cohort_var + EPSILON)
    counts_float = weight_counts.astype(jnp.float32)
    cohort_share = counts_float / jnp.sum(counts_float)
    multiplier = inv_spread * jnp.sqrt(cohort_share / cohort_size)[:, None]
    tables = [split_parts(cohort_mean), split_parts(multiplier)]

    offset = own_live * BLOCK
    placed = lax.dynamic_update_slice_in_dim(jnp.zeros_like(coded), surplus, offset, 0)
    row_index = lax.broadcasted_iota(jnp.int32, (kept, 1), 0)
    balanced = jnp.where(row_index < offset, coded[:kept], placed[:kept])
    if early:
        balanced = after(balanced, below[2], above[2])
    if not early:
        pieces = {0: standardized(balanced, tables)}
        for bit in bits:
            pieces |= {m ^ bit: swapped(block, bit) for m, block in pieces.items()}
        groups = []
        for m in range(0, n_samp, 2):
            cols = [(pieces[i], 0, kept) for i in (m, m + 1)]
            rows = along_line(jnp.concatenate([row_part(p, 0, kept) for p, _, _ in cols], 0))
            if n_var > 4:
                rows = [rows[0], sum(rows[2:], rows[1])]
            groups.append((cols, [rows]))
        return gram_of(groups, role, 3)

    def of_panel(panel):
        chosen = jnp.zeros_like(below[0])
        for h in range(1, n_var):
            chosen += jnp.where(panel == var - h, below[h], jnp.zeros_like(below[h]))
            chosen += jnp.where(panel == var + h, above[h], jnp.zeros_like(above[h]))
        return chosen

    chip = samp // 2
    far, near, both = 4, 2, 6
    size, used = kept - early, PARTS * COHORTS
    rest = lambda m: pieces[m][early:]
    panel = lambda got: jnp.where(owns_rows, got[0], sum(got[2:], got[1]))
    other_half = lambda block: lax.dynamic_slice_in_dim(block, height - row_start, height, 1)
    my_half = lambda block: row_part(block, 0, block.shape[0])

    sent_tables = jnp.concatenate([t[:used] for t in tables], 0)
    base, first = standardized(balanced, tables, sent_tables, early)
    pieces = {0: base}
    pieces[far], pieces[near] = swapped(base, far), swapped(base, near)
    legs = [along_line(first)]
    pieces[1] = swapped(base, 1)
    legs.append(along_line(after(rest(near), pieces[1], below[3], above[3], legs[0][1], pieces[far])))
    pieces[both] = swapped(after(pieces[far], pieces[near], legs[0][1]), near)
    legs.append(along_line(after(rest(far), legs[0][1])))
    up = jnp.concatenate([of_panel(chip ^ 2), of_panel(chip ^ 3)], 0)
    up = swapped(after(up, legs[1][1]), far)
    pieces[both + 1] = swapped(after(pieces[both], *legs[0][2:], legs[1][1]), 1)
    done = (legs[2][1], *legs[1][2:])
    tail = [row_part(pieces[m], early, size) for m in (both, both + 1)]
    legs.append(along_line(after(tail[0], *done), *legs[2][2:]))
    legs.append(along_line(after(tail[1], *done), *legs[2][2:], *legs[3][2:]))
    aside = jnp.concatenate([of_panel(chip ^ 1), up[early:]], 0)
    aside = swapped(after(aside, *done), near)
    brought = jnp.concatenate([of_panel(chip), aside[:early], up[:early], aside[early:]], 0)
    other = swapped(brought, 1)
    pieces[far + 1] = swapped(after(pieces[far], pieces[both + 1]), 1)
    pieces[near + 1] = swapped(after(pieces[near], pieces[far + 1]), 1)
    whole = [panel([part[:size] for part in leg]) for leg in legs[:3]]
    others = [swapped(other_half(block), 1) for block in whole]

    row_tables = my_half(panel([part[size:] for part in legs[0]]))
    pad = jnp.zeros((TABLE - used, height), jnp.bfloat16)
    row_tables = [jnp.concatenate([row_tables[i : i + used], pad], 0) for i in (0, used)]
    order = [*range(0, n_samp, 2), *range(1, n_samp, 2)]
    source = samp ^ jnp.asarray(order, jnp.int32)
    pick = (source[:, None] == jnp.arange(n_samp)[None, :]).astype(jnp.float32)
    early_codes = jnp.dot(pick, sums[:n_samp, width + TABLE : width + TABLE + early])
    lanes = jnp.broadcast_to(early_codes.reshape(-1, 1), (n_samp * early, TABLE))
    brought = jnp.concatenate([my_half(brought), my_half(other)], 0)
    brought = standardized(jnp.concatenate([brought, lanes.astype(jnp.bfloat16)], 1), row_tables)
    own = jnp.concatenate([row_part(pieces[m], 0, early) for m in order], 0)

    cols = lambda *ms: [(pieces[m], early, size) for m in ms]
    groups = [([(pieces[m], 0, early) for m in order], [[own, brought]])]
    groups += [
        (cols(i, i + 1), [[my_half(block)], [other]])
        for i, block, other in zip((0, near, far), whole, others)
    ]
    groups.append((cols(both, both + 1), legs[3:]))
    return gram_of(groups, role, 4)


def solution(mesh):
    placed = (P("samp", "var"), P("samp"), P("samp"), P())
    return jax.shard_map(
        shards, mesh=mesh, in_specs=placed, out_specs=P("samp", "var"), check_vma=False
    )
```

```python
import functools

import jax
import jax.numpy as jnp
from jax import lax
from jax.experimental import pallas as pl
from jax.experimental.pallas import tpu as pltpu
from jax.sharding import PartitionSpec as P

COHORTS = 8
BLOCK = 96
HALF = 4
EPSILON = 1e-05
PARTS = 3
TABLE = 128


def swapped(block, distance):
    return lax.ppermute(
        block, "samp", [(i, i ^ distance) for i in range(lax.axis_size("samp"))]
    )


def hops(owner, count):
    if count == 4:
        low = owner < 2
        middle = 2 if low else 1
        ends = [p for p in range(4) if p not in (owner, middle)]
        ends.sort(reverse=low)
        return [(0, owner, middle)] + [(i + 1, middle, e) for i, e in enumerate(ends)]
    down, up = list(range(owner - 1, -1, -1)), list(range(owner + 1, count))
    visited = [owner] + (down + up if owner < count // 2 else up + down)
    return [(i, visited[i], visited[i + 1]) for i in range(count - 1)]


def split_parts(table):
    parts, rest = [], table
    for _ in range(PARTS):
        part = lax.reduce_precision(rest, exponent_bits=8, mantissa_bits=7)
        parts.append(part.astype(jnp.bfloat16))
        rest = rest - part
    used = PARTS * COHORTS
    parts.append(jnp.zeros((TABLE - used, table.shape[1]), jnp.bfloat16))
    return jnp.concatenate(parts, 0)


def sums_kernel(member_ref, dose_ref, sums_ref):
    member = member_ref[...]
    dose = dose_ref[...]
    wide = dose.astype(jnp.float32)
    square = wide * wide
    high = square.astype(jnp.bfloat16)
    low = (square - high.astype(jnp.float32)).astype(jnp.bfloat16)
    dot = functools.partial(jnp.dot, preferred_element_type=jnp.float32)
    sums_ref[:COHORTS, :] = dot(member, dose)[:COHORTS]
    sums_ref[COHORTS:, :] = (dot(member, high) + dot(member, low))[:COHORTS]


def cohort_sums(member, dose):
    rows, columns = dose.shape
    tile = min(512, columns)
    return pl.pallas_call(
        sums_kernel,
        grid=(columns // tile,),
        in_specs=[
            pl.BlockSpec((16, rows), lambda j: (0, 0)),
            pl.BlockSpec((rows, tile), lambda j: (0, j)),
        ],
        out_specs=pl.BlockSpec((2 * COHORTS, tile), lambda j: (0, j)),
        out_shape=jax.ShapeDtypeStruct((2 * COHORTS, columns), jnp.float32),
        cost_estimate=pl.CostEstimate(
            flops=6 * 16 * rows * columns, bytes_accessed=2 * rows * columns, transcendentals=0
        ),
        compiler_params=pltpu.CompilerParams(vmem_limit_bytes=24 * 2**20),
    )(member, dose)


def standardize_kernel(skip, dose_ref, code_ref, mean_ref, scale_ref, *refs):
    code = code_ref[...].astype(jnp.float32)
    lane = lax.broadcasted_iota(jnp.int32, code.shape, 1)
    cohort = jnp.where(lane < PARTS * COHORTS, lane % COHORTS, -1)
    hot = (code == cohort.astype(jnp.float32)).astype(jnp.float32).astype(jnp.bfloat16)
    dot = functools.partial(jnp.dot, preferred_element_type=jnp.float32)
    centered = dose_ref[...].astype(jnp.float32) - dot(hot, mean_ref[...])
    ready = (centered * dot(hot, scale_ref[...])).astype(jnp.bfloat16)
    if len(refs) == 1:
        refs[0][...] = ready
    else:
        extra_ref, out_ref, rest_ref = refs
        kept = ready.shape[0] - skip
        out_ref[...] = ready
        rest_ref[:kept, :] = ready[skip:]
        rest_ref[kept:, :] = extra_ref[...]


def standardized(coded, tables, extra=None, skip=0):
    rows, width = coded.shape[0], coded.shape[1] - TABLE
    tile = min(512, width)
    by_tile = lambda height: pl.BlockSpec((height, tile), lambda j: (0, j))
    heights = [rows] if extra is None else [rows, rows - skip + extra.shape[0]]
    out = pl.pallas_call(
        functools.partial(standardize_kernel, skip),
        grid=(width // tile,),
        in_specs=[
            by_tile(rows),
            pl.BlockSpec((rows, TABLE), lambda j: (0, width // TABLE)),
            by_tile(TABLE),
            by_tile(TABLE),
        ]
        + ([] if extra is None else [by_tile(extra.shape[0])]),
        out_specs=[by_tile(h) for h in heights],
        out_shape=[jax.ShapeDtypeStruct((h, width), jnp.bfloat16) for h in heights],
        cost_estimate=pl.CostEstimate(
            flops=4 * TABLE * rows * width, bytes_accessed=4 * rows * width, transcendentals=0
        ),
        compiler_params=pltpu.CompilerParams(vmem_limit_bytes=24 * 2**20),
    )(coded, coded, *tables, *([] if extra is None else [extra]))
    return out[0] if extra is None else out


def gram_kernel(takes, row_sizes, row_counts, has_total, *refs):
    n = len(takes)
    role, cols, refs = refs[0][0], refs[1 : n + 1], refs[n + 1 :]
    rows = []
    for count in row_counts:
        rows.append(refs[:count])
        refs = refs[count:]
    total = refs[0] if has_total else None
    out, row_ready, col_ready, sems = refs[-4:]

    @pl.when(pl.program_id(0) == 0)
    def _():
        at, waits = 0, []
        for j, (places, size) in enumerate(zip(rows, row_sizes)):
            to = row_ready.at[pl.ds(at, size), :]
            for i, place in enumerate(places):
                here = role == i if i < len(places) - 1 else role >= i

                @pl.when(here)
                def _():
                    pltpu.make_async_copy(place, to, sems.at[j]).start()

            waits.append(pltpu.make_async_copy(places[0], to, sems.at[j]))
            at += size
        for wait in waits:
            wait.wait()

    at = 0
    for j, (start, size) in enumerate(takes):
        col_ready[at : at + size, :] = cols[j][start : start + size, :]
        at += size
    product = lax.dot_general(
        row_ready[...],
        col_ready[...],
        (((0,), (0,)), ((), ())),
        preferred_element_type=jnp.float32,
    )
    if has_total:
        product += total[...]
    out[...] = product


def gram(total, role, cols, rows):
    takes = tuple((start, size) for _, start, size in cols)
    blocks = [block for block, _, _ in cols]
    row_sizes = tuple(r[0].shape[0] for r in rows)
    depth, width, height = sum(row_sizes), blocks[0].shape[1], rows[0][0].shape[1]
    tile = min(512 if depth > height else 1024, width)
    by_tile = lambda height: pl.BlockSpec((height, tile), lambda j: (0, j))
    in_specs = (
        [pl.BlockSpec(memory_space=pltpu.SMEM)]
        + [by_tile(start + size) for start, size in takes]
        + [pl.BlockSpec(memory_space=pl.ANY) for r in rows for _ in r]
    )
    operands = [role, *blocks, *(part for r in rows for part in r)]
    aliases = {}
    if total is not None:
        aliases = {len(operands): 0}
        operands.append(total)
        in_specs.append(by_tile(height))
    return pl.pallas_call(
        functools.partial(
            gram_kernel, takes, row_sizes, tuple(len(r) for r in rows), total is not None
        ),
        grid=(width // tile,),
        in_specs=in_specs,
        out_specs=by_tile(height),
        out_shape=jax.ShapeDtypeStruct((height, width), jnp.float32),
        scratch_shapes=[
            pltpu.VMEM((depth, height), jnp.bfloat16),
            pltpu.VMEM((depth, tile), jnp.bfloat16),
            pltpu.SemaphoreType.DMA((len(rows),)),
        ],
        input_output_aliases=aliases,
        cost_estimate=pl.CostEstimate(
            flops=2 * depth * height * width,
            bytes_accessed=8 * height * width + 2 * depth * (height + width),
            transcendentals=0,
        ),
        compiler_params=pltpu.CompilerParams(vmem_limit_bytes=48 * 2**20),
    )(*operands)


def gram_of(groups, role, at_once):
    total = None
    for at in range(0, len(groups), at_once):
        part = groups[at : at + at_once]
        cols = [c for g in part for c in g[0]]
        total = gram(total, role, cols, [r for g in part for r in g[1]])
    return total


def after(block, *done):
    return lax.optimization_barrier((block, *done))[0]


def shards(dosage, cohort, live_blocks, weight_counts):
    n_samp, n_var = lax.axis_size("samp"), lax.axis_size("var")
    samp, var = lax.axis_index("samp"), lax.axis_index("var")
    slots, width = dosage.shape
    height = width * n_var // n_samp
    kept = HALF * BLOCK
    owner = [i * height // width for i in range(n_samp)]
    owns_rows = samp * height // width == var
    lines = [hops(o, n_var) for o in owner]
    reached = [[0] * n_var for _ in range(n_samp)]
    for s, line in enumerate(lines):
        for step, _, end in line:
            reached[s][end] = step + 1
    here = (jnp.arange(n_samp)[:, None] == samp) & (jnp.arange(n_var)[None, :] == var)
    role = jnp.sum(jnp.where(here, jnp.asarray(reached, jnp.int32), 0)).reshape(1)
    row_start = samp * height % width
    early = BLOCK if (n_samp, n_var) == (8, 4) else 0
    bits = [n_samp >> (b + 1) for b in range(n_samp.bit_length() - 1)]
    def hop(block, step):
        pairs = [
            (s * n_var + line[step][1], s * n_var + line[step][2]) for s, line in enumerate(lines)
        ]
        return lax.ppermute(block, ("samp", "var"), pairs)

    def along_line(block, *done):
        got = []
        for step in range(n_var - 1):
            source = [k for k in range(step) if lines[0][k][2] == lines[0][step][1]]
            moving = got[source[0]] if source else block
            got.append(hop(after(moving, *done) if source and done else moving, step))
        return [block, *got]

    def along_var(block, shift):
        pairs = [(v, v + shift) for v in range(n_var) if 0 <= v + shift < n_var]
        return lax.ppermute(block, "var", pairs)

    def row_part(block, start, size):
        return lax.dynamic_slice(block, (start, row_start), (size, height))

    own_live = live_blocks[0]
    code = cohort.astype(jnp.bfloat16)
    coded = jnp.concatenate([dosage, jnp.broadcast_to(code[:, None], (slots, TABLE))], 1)

    position = lax.broadcasted_iota(jnp.int32, (16, slots), 1)
    label = lax.broadcasted_iota(jnp.int32, (16, slots), 0)
    member = (cohort[None, :] == label) & (position < own_live * BLOCK)
    counts = jnp.sum(member.astype(jnp.float32), axis=1, keepdims=True)
    sums = cohort_sums(member.astype(jnp.bfloat16), dosage)
    extra = [jnp.broadcast_to(counts, (2 * COHORTS, TABLE))]
    if early:
        row = lax.broadcasted_iota(jnp.int32, (2 * COHORTS, early), 0)
        slot_codes = jnp.where(row == samp, cohort[None, :early].astype(jnp.float32), 0.0)
        extra.append(jnp.pad(slot_codes, ((0, 0), (0, TABLE - early))))
    sums = jnp.concatenate([sums, *extra], 1)
    surplus = swapped(coded[kept:], bits[0])
    for bit in bits[1:]:
        sums = sums + swapped(sums, bit)
    sums = sums + swapped(after(sums, surplus), bits[0])
    below, above = [dosage[:early]], [dosage[:early]]
    if early:
        for _ in range(n_var - 1):
            below.append(along_var(below[-1], 1))
            above.append(along_var(above[-1], -1))

    sum_one, sum_two = sums[:COHORTS, :width], sums[COHORTS:, :width]
    cohort_size = sums[:COHORTS, width]
    cohort_mean = sum_one / cohort_size[:, None]
    cohort_var = sum_two / cohort_size[:, None] - cohort_mean * cohort_mean
    inv_spread = lax.rsqrt(cohort_var + EPSILON)
    counts_float = weight_counts.astype(jnp.float32)
    cohort_share = counts_float / jnp.sum(counts_float)
    multiplier = inv_spread * jnp.sqrt(cohort_share / cohort_size)[:, None]
    tables = [split_parts(cohort_mean), split_parts(multiplier)]

    offset = own_live * BLOCK
    placed = lax.dynamic_update_slice_in_dim(jnp.zeros_like(coded), surplus, offset, 0)
    row_index = lax.broadcasted_iota(jnp.int32, (kept, 1), 0)
    balanced = jnp.where(row_index < offset, coded[:kept], placed[:kept])
    if early:
        balanced = after(balanced, below[2], above[2])
    if not early:
        pieces = {0: standardized(balanced, tables)}
        for bit in bits:
            pieces |= {m ^ bit: swapped(block, bit) for m, block in pieces.items()}
        groups = []
        for m in range(0, n_samp, 2):
            cols = [(pieces[i], 0, kept) for i in (m, m + 1)]
            rows = along_line(jnp.concatenate([row_part(p, 0, kept) for p, _, _ in cols], 0))
            if n_var > 4:
                rows = [rows[0], sum(rows[2:], rows[1])]
            groups.append((cols, [rows]))
        return gram_of(groups, role, 3)

    def of_panel(panel):
        chosen = jnp.zeros_like(below[0])
        for h in range(1, n_var):
            chosen += jnp.where(panel == var - h, below[h], jnp.zeros_like(below[h]))
            chosen += jnp.where(panel == var + h, above[h], jnp.zeros_like(above[h]))
        return chosen

    chip = samp // 2
    far, near, both = 4, 2, 6
    size, used = kept - early, PARTS * COHORTS
    rest = lambda m: pieces[m][early:]
    panel = lambda got: jnp.where(owns_rows, got[0], sum(got[2:], got[1]))
    other_half = lambda block: lax.dynamic_slice_in_dim(block, height - row_start, height, 1)
    my_half = lambda block: row_part(block, 0, block.shape[0])

    sent_tables = jnp.concatenate([t[:used] for t in tables], 0)
    base, first = standardized(balanced, tables, sent_tables, early)
    pieces = {0: base}
    pieces[far], pieces[near] = swapped(base, far), swapped(base, near)
    legs = [along_line(first)]
    pieces[1] = swapped(base, 1)
    legs.append(along_line(after(rest(near), pieces[1], below[3], above[3], legs[0][1], pieces[far])))
    pieces[both] = swapped(after(pieces[far], pieces[near], legs[0][1]), near)
    legs.append(along_line(after(rest(far), legs[0][1])))
    up = jnp.concatenate([of_panel(chip ^ 2), of_panel(chip ^ 3)], 0)
    up = swapped(after(up, legs[1][1]), far)
    pieces[both + 1] = swapped(after(pieces[both], *legs[0][2:], legs[1][1]), 1)
    done = (legs[2][1], *legs[1][2:])
    tail = [row_part(pieces[m], early, size) for m in (both, both + 1)]
    legs.append(along_line(after(tail[0], *done), *legs[2][2:]))
    legs.append(along_line(after(tail[1], *done), *legs[2][2:], *legs[3][2:]))
    aside = jnp.concatenate([of_panel(chip ^ 1), up[early:]], 0)
    aside = swapped(after(aside, *done), near)
    brought = jnp.concatenate([of_panel(chip), aside[:early], up[:early], aside[early:]], 0)
    other = swapped(brought, 1)
    pieces[far + 1] = swapped(after(pieces[far], pieces[both + 1]), 1)
    pieces[near + 1] = swapped(after(pieces[near], pieces[far + 1]), 1)
    whole = [panel([part[:size] for part in leg]) for leg in legs[:3]]
    others = [swapped(other_half(block), 1) for block in whole]

    row_tables = my_half(panel([part[size:] for part in legs[0]]))
    pad = jnp.zeros((TABLE - used, height), jnp.bfloat16)
    row_tables = [jnp.concatenate([row_tables[i : i + used], pad], 0) for i in (0, used)]
    order = [*range(0, n_samp, 2), *range(1, n_samp, 2)]
    source = samp ^ jnp.asarray(order, jnp.int32)
    pick = (source[:, None] == jnp.arange(n_samp)[None, :]).astype(jnp.float32)
    early_codes = jnp.dot(pick, sums[:n_samp, width + TABLE : width + TABLE + early])
    lanes = jnp.broadcast_to(early_codes.reshape(-1, 1), (n_samp * early, TABLE))
    brought = jnp.concatenate([my_half(brought), my_half(other)], 0)
    brought = standardized(jnp.concatenate([brought, lanes.astype(jnp.bfloat16)], 1), row_tables)
    own = jnp.concatenate([row_part(pieces[m], 0, early) for m in order], 0)

    cols = lambda *ms: [(pieces[m], early, size) for m in ms]
    groups = [([(pieces[m], 0, early) for m in order], [[own, brought]])]
    groups += [
        (cols(i, i + 1), [[my_half(block)], [other]])
        for i, block, other in zip((0, near, far), whole, others)
    ]
    groups.append((cols(both, both + 1), legs[3:]))
    return gram_of(groups, role, 4)


def solution(mesh):
    placed = (P("samp", "var"), P("samp"), P("samp"), P())
    return jax.shard_map(
        shards, mesh=mesh, in_specs=placed, out_specs=P("samp", "var"), check_vma=False
    )
```

```python
import functools

import jax
import jax.numpy as jnp
from jax import lax
from jax.experimental import pallas as pl
from jax.experimental.pallas import tpu as pltpu
from jax.sharding import PartitionSpec as P

COHORTS = 8
BLOCK = 96
HALF = 4
EPSILON = 1e-05
PARTS = 3
TABLE = 128


def swapped(block, distance):
    return lax.ppermute(
        block, "samp", [(i, i ^ distance) for i in range(lax.axis_size("samp"))]
    )


def hops(owner, count):
    if count == 4:
        low = owner < 2
        middle = 2 if low else 1
        ends = [p for p in range(4) if p not in (owner, middle)]
        ends.sort(reverse=low)
        return [(0, owner, middle)] + [(i + 1, middle, e) for i, e in enumerate(ends)]
    down, up = list(range(owner - 1, -1, -1)), list(range(owner + 1, count))
    visited = [owner] + (down + up if owner < count // 2 else up + down)
    return [(i, visited[i], visited[i + 1]) for i in range(count - 1)]


def split_parts(table):
    parts, rest = [], table
    for _ in range(PARTS):
        part = lax.reduce_precision(rest, exponent_bits=8, mantissa_bits=7)
        parts.append(part.astype(jnp.bfloat16))
        rest = rest - part
    used = PARTS * COHORTS
    parts.append(jnp.zeros((TABLE - used, table.shape[1]), jnp.bfloat16))
    return jnp.concatenate(parts, 0)


def sums_kernel(member_ref, dose_ref, sums_ref):
    member = member_ref[...]
    dose = dose_ref[...]
    wide = dose.astype(jnp.float32)
    square = wide * wide
    high = square.astype(jnp.bfloat16)
    low = (square - high.astype(jnp.float32)).astype(jnp.bfloat16)
    dot = functools.partial(jnp.dot, preferred_element_type=jnp.float32)
    sums_ref[:COHORTS, :] = dot(member, dose)[:COHORTS]
    sums_ref[COHORTS:, :] = (dot(member, high) + dot(member, low))[:COHORTS]


def cohort_sums(member, dose):
    rows, columns = dose.shape
    tile = min(512, columns)
    return pl.pallas_call(
        sums_kernel,
        grid=(columns // tile,),
        in_specs=[
            pl.BlockSpec((16, rows), lambda j: (0, 0)),
            pl.BlockSpec((rows, tile), lambda j: (0, j)),
        ],
        out_specs=pl.BlockSpec((2 * COHORTS, tile), lambda j: (0, j)),
        out_shape=jax.ShapeDtypeStruct((2 * COHORTS, columns), jnp.float32),
        cost_estimate=pl.CostEstimate(
            flops=6 * 16 * rows * columns, bytes_accessed=2 * rows * columns, transcendentals=0
        ),
        compiler_params=pltpu.CompilerParams(vmem_limit_bytes=24 * 2**20),
    )(member, dose)


def standardize_kernel(skip, dose_ref, code_ref, mean_ref, scale_ref, *refs):
    code = code_ref[...].astype(jnp.float32)
    lane = lax.broadcasted_iota(jnp.int32, code.shape, 1)
    cohort = jnp.where(lane < PARTS * COHORTS, lane % COHORTS, -1)
    hot = (code == cohort.astype(jnp.float32)).astype(jnp.float32).astype(jnp.bfloat16)
    dot = functools.partial(jnp.dot, preferred_element_type=jnp.float32)
    centered = dose_ref[...].astype(jnp.float32) - dot(hot, mean_ref[...])
    ready = (centered * dot(hot, scale_ref[...])).astype(jnp.bfloat16)
    if len(refs) == 1:
        refs[0][...] = ready
    else:
        extra_ref, out_ref, rest_ref = refs
        kept = ready.shape[0] - skip
        out_ref[...] = ready
        rest_ref[:kept, :] = ready[skip:]
        rest_ref[kept:, :] = extra_ref[...]


def standardized(coded, tables, extra=None, skip=0):
    rows, width = coded.shape[0], coded.shape[1] - TABLE
    tile = min(512, width)
    by_tile = lambda height: pl.BlockSpec((height, tile), lambda j: (0, j))
    heights = [rows] if extra is None else [rows, rows - skip + extra.shape[0]]
    out = pl.pallas_call(
        functools.partial(standardize_kernel, skip),
        grid=(width // tile,),
        in_specs=[
            by_tile(rows),
            pl.BlockSpec((rows, TABLE), lambda j: (0, width // TABLE)),
            by_tile(TABLE),
            by_tile(TABLE),
        ]
        + ([] if extra is None else [by_tile(extra.shape[0])]),
        out_specs=[by_tile(h) for h in heights],
        out_shape=[jax.ShapeDtypeStruct((h, width), jnp.bfloat16) for h in heights],
        cost_estimate=pl.CostEstimate(
            flops=4 * TABLE * rows * width, bytes_accessed=4 * rows * width, transcendentals=0
        ),
        compiler_params=pltpu.CompilerParams(vmem_limit_bytes=24 * 2**20),
    )(coded, coded, *tables, *([] if extra is None else [extra]))
    return out[0] if extra is None else out


def gram_kernel(takes, row_sizes, row_counts, has_total, *refs):
    n = len(takes)
    role, cols, refs = refs[0][0], refs[1 : n + 1], refs[n + 1 :]
    rows = []
    for count in row_counts:
        rows.append(refs[:count])
        refs = refs[count:]
    total = refs[0] if has_total else None
    out, row_ready, col_ready, sems = refs[-4:]

    first = pl.program_id(0) == 0

    @pl.when(first)
    def _():
        at = 0
        for j, (places, size) in enumerate(zip(rows, row_sizes)):
            to = row_ready.at[pl.ds(at, size), :]
            for i, place in enumerate(places):
                here = role == i if i < len(places) - 1 else role >= i

                @pl.when(here)
                def _():
                    pltpu.make_async_copy(place, to, sems.at[j]).start()

            at += size

    at = 0
    for j, (start, size) in enumerate(takes):
        col_ready[at : at + size, :] = cols[j][start : start + size, :]
        at += size

    @pl.when(first)
    def _():
        at = 0
        for j, (places, size) in enumerate(zip(rows, row_sizes)):
            to = row_ready.at[pl.ds(at, size), :]
            pltpu.make_async_copy(places[0], to, sems.at[j]).wait()
            at += size

    product = lax.dot_general(
        row_ready[...],
        col_ready[...],
        (((0,), (0,)), ((), ())),
        preferred_element_type=jnp.float32,
    )
    if has_total:
        product += total[...]
    out[...] = product


def gram(total, role, cols, rows):
    takes = tuple((start, size) for _, start, size in cols)
    blocks = [block for block, _, _ in cols]
    row_sizes = tuple(r[0].shape[0] for r in rows)
    depth, width, height = sum(row_sizes), blocks[0].shape[1], rows[0][0].shape[1]
    tile = min(512 if depth > height else 1024, width)
    by_tile = lambda height: pl.BlockSpec((height, tile), lambda j: (0, j))
    in_specs = (
        [pl.BlockSpec(memory_space=pltpu.SMEM)]
        + [by_tile(start + size) for start, size in takes]
        + [pl.BlockSpec(memory_space=pl.ANY) for r in rows for _ in r]
    )
    operands = [role, *blocks, *(part for r in rows for part in r)]
    aliases = {}
    if total is not None:
        aliases = {len(operands): 0}
        operands.append(total)
        in_specs.append(by_tile(height))
    return pl.pallas_call(
        functools.partial(
            gram_kernel, takes, row_sizes, tuple(len(r) for r in rows), total is not None
        ),
        grid=(width // tile,),
        in_specs=in_specs,
        out_specs=by_tile(height),
        out_shape=jax.ShapeDtypeStruct((height, width), jnp.float32),
        scratch_shapes=[
            pltpu.VMEM((depth, height), jnp.bfloat16),
            pltpu.VMEM((depth, tile), jnp.bfloat16),
            pltpu.SemaphoreType.DMA((len(rows),)),
        ],
        input_output_aliases=aliases,
        cost_estimate=pl.CostEstimate(
            flops=2 * depth * height * width,
            bytes_accessed=8 * height * width + 2 * depth * (height + width),
            transcendentals=0,
        ),
        compiler_params=pltpu.CompilerParams(vmem_limit_bytes=48 * 2**20),
    )(*operands)


def gram_of(groups, role, at_once):
    total = None
    for at in range(0, len(groups), at_once):
        part = groups[at : at + at_once]
        cols = [c for g in part for c in g[0]]
        total = gram(total, role, cols, [r for g in part for r in g[1]])
    return total


def after(block, *done):
    return lax.optimization_barrier((block, *done))[0]


def shards(dosage, cohort, live_blocks, weight_counts):
    n_samp, n_var = lax.axis_size("samp"), lax.axis_size("var")
    samp, var = lax.axis_index("samp"), lax.axis_index("var")
    slots, width = dosage.shape
    height = width * n_var // n_samp
    kept = HALF * BLOCK
    owner = [i * height // width for i in range(n_samp)]
    owns_rows = samp * height // width == var
    lines = [hops(o, n_var) for o in owner]
    reached = [[0] * n_var for _ in range(n_samp)]
    for s, line in enumerate(lines):
        for step, _, end in line:
            reached[s][end] = step + 1
    here = (jnp.arange(n_samp)[:, None] == samp) & (jnp.arange(n_var)[None, :] == var)
    role = jnp.sum(jnp.where(here, jnp.asarray(reached, jnp.int32), 0)).reshape(1)
    row_start = samp * height % width
    early = BLOCK if (n_samp, n_var) == (8, 4) else 0
    bits = [n_samp >> (b + 1) for b in range(n_samp.bit_length() - 1)]
    def hop(block, step):
        pairs = [
            (s * n_var + line[step][1], s * n_var + line[step][2]) for s, line in enumerate(lines)
        ]
        return lax.ppermute(block, ("samp", "var"), pairs)

    def along_line(block, *done):
        got = []
        for step in range(n_var - 1):
            source = [k for k in range(step) if lines[0][k][2] == lines[0][step][1]]
            moving = got[source[0]] if source else block
            got.append(hop(after(moving, *done) if source and done else moving, step))
        return [block, *got]

    def along_var(block, shift):
        pairs = [(v, v + shift) for v in range(n_var) if 0 <= v + shift < n_var]
        return lax.ppermute(block, "var", pairs)

    def row_part(block, start, size):
        return lax.dynamic_slice(block, (start, row_start), (size, height))

    own_live = live_blocks[0]
    code = cohort.astype(jnp.bfloat16)
    coded = jnp.concatenate([dosage, jnp.broadcast_to(code[:, None], (slots, TABLE))], 1)

    position = lax.broadcasted_iota(jnp.int32, (16, slots), 1)
    label = lax.broadcasted_iota(jnp.int32, (16, slots), 0)
    member = (cohort[None, :] == label) & (position < own_live * BLOCK)
    counts = jnp.sum(member.astype(jnp.float32), axis=1, keepdims=True)
    sums = cohort_sums(member.astype(jnp.bfloat16), dosage)
    extra = [jnp.broadcast_to(counts, (2 * COHORTS, TABLE))]
    if early:
        row = lax.broadcasted_iota(jnp.int32, (2 * COHORTS, early), 0)
        slot_codes = jnp.where(row == samp, cohort[None, :early].astype(jnp.float32), 0.0)
        extra.append(jnp.pad(slot_codes, ((0, 0), (0, TABLE - early))))
    sums = jnp.concatenate([sums, *extra], 1)
    surplus = swapped(coded[kept:], bits[0])
    for bit in bits[1:]:
        sums = sums + swapped(sums, bit)
    sums = sums + swapped(after(sums, surplus), bits[0])
    below, above = [dosage[:early]], [dosage[:early]]
    if early:
        for _ in range(n_var - 1):
            below.append(along_var(below[-1], 1))
            above.append(along_var(above[-1], -1))

    sum_one, sum_two = sums[:COHORTS, :width], sums[COHORTS:, :width]
    cohort_size = sums[:COHORTS, width]
    cohort_mean = sum_one / cohort_size[:, None]
    cohort_var = sum_two / cohort_size[:, None] - cohort_mean * cohort_mean
    inv_spread = lax.rsqrt(cohort_var + EPSILON)
    counts_float = weight_counts.astype(jnp.float32)
    cohort_share = counts_float / jnp.sum(counts_float)
    multiplier = inv_spread * jnp.sqrt(cohort_share / cohort_size)[:, None]
    tables = [split_parts(cohort_mean), split_parts(multiplier)]

    offset = own_live * BLOCK
    placed = lax.dynamic_update_slice_in_dim(jnp.zeros_like(coded), surplus, offset, 0)
    row_index = lax.broadcasted_iota(jnp.int32, (kept, 1), 0)
    balanced = jnp.where(row_index < offset, coded[:kept], placed[:kept])
    if early:
        balanced = after(balanced, below[2], above[2])
    if not early:
        pieces = {0: standardized(balanced, tables)}
        for bit in bits:
            pieces |= {m ^ bit: swapped(block, bit) for m, block in pieces.items()}
        groups = []
        for m in range(0, n_samp, 2):
            cols = [(pieces[i], 0, kept) for i in (m, m + 1)]
            rows = along_line(jnp.concatenate([row_part(p, 0, kept) for p, _, _ in cols], 0))
            if n_var > 4:
                rows = [rows[0], sum(rows[2:], rows[1])]
            groups.append((cols, [rows]))
        return gram_of(groups, role, 3)

    def of_panel(panel):
        chosen = jnp.zeros_like(below[0])
        for h in range(1, n_var):
            chosen += jnp.where(panel == var - h, below[h], jnp.zeros_like(below[h]))
            chosen += jnp.where(panel == var + h, above[h], jnp.zeros_like(above[h]))
        return chosen

    chip = samp // 2
    far, near, both = 4, 2, 6
    size, used = kept - early, PARTS * COHORTS
    rest = lambda m: pieces[m][early:]
    panel = lambda got: jnp.where(owns_rows, got[0], sum(got[2:], got[1]))
    other_half = lambda block: lax.dynamic_slice_in_dim(block, height - row_start, height, 1)
    my_half = lambda block: row_part(block, 0, block.shape[0])

    sent_tables = jnp.concatenate([t[:used] for t in tables], 0)
    base, first = standardized(balanced, tables, sent_tables, early)
    pieces = {0: base}
    pieces[far], pieces[near] = swapped(base, far), swapped(base, near)
    legs = [along_line(first)]
    pieces[1] = swapped(base, 1)
    legs.append(along_line(after(rest(near), pieces[1], below[3], above[3], legs[0][1], pieces[far])))
    pieces[both] = swapped(after(pieces[far], pieces[near], legs[0][1]), near)
    legs.append(along_line(after(rest(far), legs[0][1])))
    up = jnp.concatenate([of_panel(chip ^ 2), of_panel(chip ^ 3)], 0)
    up = swapped(after(up, legs[1][1]), far)
    pieces[both + 1] = swapped(after(pieces[both], *legs[0][2:], legs[1][1]), 1)
    done = (legs[2][1], *legs[1][2:])
    tail = [row_part(pieces[m], early, size) for m in (both, both + 1)]
    legs.append(along_line(after(tail[0], *done), *legs[2][2:]))
    legs.append(along_line(after(tail[1], *done), *legs[2][2:], *legs[3][2:]))
    aside = jnp.concatenate([of_panel(chip ^ 1), up[early:]], 0)
    aside = swapped(after(aside, *done), near)
    brought = jnp.concatenate([of_panel(chip), aside[:early], up[:early], aside[early:]], 0)
    other = swapped(brought, 1)
    pieces[far + 1] = swapped(after(pieces[far], pieces[both + 1]), 1)
    pieces[near + 1] = swapped(after(pieces[near], pieces[far + 1]), 1)
    whole = [panel([part[:size] for part in leg]) for leg in legs[:3]]
    others = [swapped(other_half(block), 1) for block in whole]

    row_tables = my_half(panel([part[size:] for part in legs[0]]))
    pad = jnp.zeros((TABLE - used, height), jnp.bfloat16)
    row_tables = [jnp.concatenate([row_tables[i : i + used], pad], 0) for i in (0, used)]
    order = [*range(0, n_samp, 2), *range(1, n_samp, 2)]
    source = samp ^ jnp.asarray(order, jnp.int32)
    pick = (source[:, None] == jnp.arange(n_samp)[None, :]).astype(jnp.float32)
    early_codes = jnp.dot(pick, sums[:n_samp, width + TABLE : width + TABLE + early])
    lanes = jnp.broadcast_to(early_codes.reshape(-1, 1), (n_samp * early, TABLE))
    brought = jnp.concatenate([my_half(brought), my_half(other)], 0)
    brought = standardized(jnp.concatenate([brought, lanes.astype(jnp.bfloat16)], 1), row_tables)
    own = jnp.concatenate([row_part(pieces[m], 0, early) for m in order], 0)

    cols = lambda *ms: [(pieces[m], early, size) for m in ms]
    groups = [([(pieces[m], 0, early) for m in order], [[own, brought]])]
    groups += [
        (cols(i, i + 1), [[my_half(block)], [other]])
        for i, block, other in zip((0, near, far), whole, others)
    ]
    groups.append((cols(both, both + 1), legs[3:]))
    return gram_of(groups, role, 4)


def solution(mesh):
    placed = (P("samp", "var"), P("samp"), P("samp"), P())
    return jax.shard_map(
        shards, mesh=mesh, in_specs=placed, out_specs=P("samp", "var"), check_vma=False
    )
```

```python
import functools

import jax
import jax.numpy as jnp
from jax import lax
from jax.experimental import pallas as pl
from jax.experimental.pallas import tpu as pltpu
from jax.sharding import PartitionSpec as P

COHORTS = 8
BLOCK = 96
HALF = 4
EPSILON = 1e-05
PARTS = 3
TABLE = 128


def swapped(block, distance):
    return lax.ppermute(
        block, "samp", [(i, i ^ distance) for i in range(lax.axis_size("samp"))]
    )


def hops(owner, count):
    if count == 4:
        low = owner < 2
        middle = 2 if low else 1
        ends = [p for p in range(4) if p not in (owner, middle)]
        ends.sort(reverse=low)
        return [(0, owner, middle)] + [(i + 1, middle, e) for i, e in enumerate(ends)]
    down, up = list(range(owner - 1, -1, -1)), list(range(owner + 1, count))
    visited = [owner] + (down + up if owner < count // 2 else up + down)
    return [(i, visited[i], visited[i + 1]) for i in range(count - 1)]


def split_parts(table):
    parts, rest = [], table
    for _ in range(PARTS):
        part = lax.reduce_precision(rest, exponent_bits=8, mantissa_bits=7)
        parts.append(part.astype(jnp.bfloat16))
        rest = rest - part
    used = PARTS * COHORTS
    parts.append(jnp.zeros((TABLE - used, table.shape[1]), jnp.bfloat16))
    return jnp.concatenate(parts, 0)


def sums_kernel(member_ref, dose_ref, sums_ref):
    member = member_ref[...]
    dose = dose_ref[...]
    wide = dose.astype(jnp.float32)
    square = wide * wide
    high = square.astype(jnp.bfloat16)
    low = (square - high.astype(jnp.float32)).astype(jnp.bfloat16)
    dot = functools.partial(jnp.dot, preferred_element_type=jnp.float32)
    sums_ref[:COHORTS, :] = dot(member, dose)[:COHORTS]
    sums_ref[COHORTS:, :] = (dot(member, high) + dot(member, low))[:COHORTS]


def cohort_sums(member, dose):
    rows, columns = dose.shape
    tile = min(512, columns)
    return pl.pallas_call(
        sums_kernel,
        grid=(columns // tile,),
        in_specs=[
            pl.BlockSpec((16, rows), lambda j: (0, 0)),
            pl.BlockSpec((rows, tile), lambda j: (0, j)),
        ],
        out_specs=pl.BlockSpec((2 * COHORTS, tile), lambda j: (0, j)),
        out_shape=jax.ShapeDtypeStruct((2 * COHORTS, columns), jnp.float32),
        cost_estimate=pl.CostEstimate(
            flops=6 * 16 * rows * columns, bytes_accessed=2 * rows * columns, transcendentals=0
        ),
        compiler_params=pltpu.CompilerParams(vmem_limit_bytes=24 * 2**20),
    )(member, dose)


def standardize_kernel(skip, dose_ref, code_ref, mean_ref, scale_ref, *refs):
    code = code_ref[...].astype(jnp.float32)
    lane = lax.broadcasted_iota(jnp.int32, code.shape, 1)
    cohort = jnp.where(lane < PARTS * COHORTS, lane % COHORTS, -1)
    hot = (code == cohort.astype(jnp.float32)).astype(jnp.float32).astype(jnp.bfloat16)
    dot = functools.partial(jnp.dot, preferred_element_type=jnp.float32)
    centered = dose_ref[...].astype(jnp.float32) - dot(hot, mean_ref[...])
    ready = (centered * dot(hot, scale_ref[...])).astype(jnp.bfloat16)
    if len(refs) == 1:
        refs[0][...] = ready
    else:
        extra_ref, out_ref, rest_ref = refs
        kept = ready.shape[0] - skip
        out_ref[...] = ready
        rest_ref[:kept, :] = ready[skip:]
        rest_ref[kept:, :] = extra_ref[...]


def standardized(coded, tables, extra=None, skip=0):
    rows, width = coded.shape[0], coded.shape[1] - TABLE
    tile = min(512, width)
    by_tile = lambda height: pl.BlockSpec((height, tile), lambda j: (0, j))
    heights = [rows] if extra is None else [rows, rows - skip + extra.shape[0]]
    out = pl.pallas_call(
        functools.partial(standardize_kernel, skip),
        grid=(width // tile,),
        in_specs=[
            by_tile(rows),
            pl.BlockSpec((rows, TABLE), lambda j: (0, width // TABLE)),
            by_tile(TABLE),
            by_tile(TABLE),
        ]
        + ([] if extra is None else [by_tile(extra.shape[0])]),
        out_specs=[by_tile(h) for h in heights],
        out_shape=[jax.ShapeDtypeStruct((h, width), jnp.bfloat16) for h in heights],
        cost_estimate=pl.CostEstimate(
            flops=4 * TABLE * rows * width, bytes_accessed=4 * rows * width, transcendentals=0
        ),
        compiler_params=pltpu.CompilerParams(vmem_limit_bytes=24 * 2**20),
    )(coded, coded, *tables, *([] if extra is None else [extra]))
    return out[0] if extra is None else out


def gram_kernel(takes, row_sizes, row_counts, has_total, *refs):
    n = len(takes)
    role, cols, refs = refs[0][0], refs[1 : n + 1], refs[n + 1 :]
    rows = []
    for count in row_counts:
        rows.append(refs[:count])
        refs = refs[count:]
    total = refs[0] if has_total else None
    out, row_ready, col_ready, sems = refs[-4:]

    @pl.when(pl.program_id(0) == 0)
    def _():
        at, waits = 0, []
        for j, (places, size) in enumerate(zip(rows, row_sizes)):
            to = row_ready.at[pl.ds(at, size), :]
            for i, place in enumerate(places):
                here = role == i if i < len(places) - 1 else role >= i

                @pl.when(here)
                def _():
                    pltpu.make_async_copy(place, to, sems.at[j]).start()

            waits.append(pltpu.make_async_copy(places[0], to, sems.at[j]))
            at += size
        for wait in waits:
            wait.wait()

    at = 0
    for j, (start, size) in enumerate(takes):
        col_ready[at : at + size, :] = cols[j][start : start + size, :]
        at += size
    product = lax.dot_general(
        row_ready[...],
        col_ready[...],
        (((0,), (0,)), ((), ())),
        preferred_element_type=jnp.float32,
    )
    if has_total:
        product += total[...]
    out[...] = product


def gram(total, role, cols, rows):
    takes = tuple((start, size) for _, start, size in cols)
    blocks = [block for block, _, _ in cols]
    row_sizes = tuple(r[0].shape[0] for r in rows)
    depth, width, height = sum(row_sizes), blocks[0].shape[1], rows[0][0].shape[1]
    tile = min(512 if depth > height else 1024, width)
    by_tile = lambda height: pl.BlockSpec((height, tile), lambda j: (0, j))
    in_specs = (
        [pl.BlockSpec(memory_space=pltpu.SMEM)]
        + [by_tile(start + size) for start, size in takes]
        + [pl.BlockSpec(memory_space=pl.ANY) for r in rows for _ in r]
    )
    operands = [role, *blocks, *(part for r in rows for part in r)]
    aliases = {}
    if total is not None:
        aliases = {len(operands): 0}
        operands.append(total)
        in_specs.append(by_tile(height))
    return pl.pallas_call(
        functools.partial(
            gram_kernel, takes, row_sizes, tuple(len(r) for r in rows), total is not None
        ),
        grid=(width // tile,),
        in_specs=in_specs,
        out_specs=by_tile(height),
        out_shape=jax.ShapeDtypeStruct((height, width), jnp.float32),
        scratch_shapes=[
            pltpu.VMEM((depth, height), jnp.bfloat16),
            pltpu.VMEM((depth, tile), jnp.bfloat16),
            pltpu.SemaphoreType.DMA((len(rows),)),
        ],
        input_output_aliases=aliases,
        cost_estimate=pl.CostEstimate(
            flops=2 * depth * height * width,
            bytes_accessed=8 * height * width + 2 * depth * (height + width),
            transcendentals=0,
        ),
        compiler_params=pltpu.CompilerParams(vmem_limit_bytes=48 * 2**20),
    )(*operands)


def gram_of(groups, role, at_once):
    total = None
    for at in range(0, len(groups), at_once):
        part = groups[at : at + at_once]
        cols = [c for g in part for c in g[0]]
        total = gram(total, role, cols, [r for g in part for r in g[1]])
    return total


def after(block, *done):
    return lax.optimization_barrier((block, *done))[0]


def shards(dosage, cohort, live_blocks, weight_counts):
    n_samp, n_var = lax.axis_size("samp"), lax.axis_size("var")
    samp, var = lax.axis_index("samp"), lax.axis_index("var")
    slots, width = dosage.shape
    height = width * n_var // n_samp
    kept = HALF * BLOCK
    owner = [i * height // width for i in range(n_samp)]
    owns_rows = samp * height // width == var
    lines = [hops(o, n_var) for o in owner]
    reached = [[0] * n_var for _ in range(n_samp)]
    for s, line in enumerate(lines):
        for step, _, end in line:
            reached[s][end] = step + 1
    here = (jnp.arange(n_samp)[:, None] == samp) & (jnp.arange(n_var)[None, :] == var)
    role = jnp.sum(jnp.where(here, jnp.asarray(reached, jnp.int32), 0)).reshape(1)
    row_start = samp * height % width
    early = BLOCK if (n_samp, n_var) == (8, 4) else 0
    bits = [n_samp >> (b + 1) for b in range(n_samp.bit_length() - 1)]
    def hop(block, step):
        pairs = [
            (s * n_var + line[step][1], s * n_var + line[step][2]) for s, line in enumerate(lines)
        ]
        return lax.ppermute(block, ("samp", "var"), pairs)

    def along_line(block, *done):
        got = []
        for step in range(n_var - 1):
            source = [k for k in range(step) if lines[0][k][2] == lines[0][step][1]]
            moving = got[source[0]] if source else block
            got.append(hop(after(moving, *done) if source and done else moving, step))
        return [block, *got]

    def along_var(block, shift):
        pairs = [(v, v + shift) for v in range(n_var) if 0 <= v + shift < n_var]
        return lax.ppermute(block, "var", pairs)

    def row_part(block, start, size):
        return lax.dynamic_slice(block, (start, row_start), (size, height))

    own_live = live_blocks[0]
    code = cohort.astype(jnp.bfloat16)
    coded = jnp.concatenate([dosage, jnp.broadcast_to(code[:, None], (slots, TABLE))], 1)

    position = lax.broadcasted_iota(jnp.int32, (16, slots), 1)
    label = lax.broadcasted_iota(jnp.int32, (16, slots), 0)
    member = (cohort[None, :] == label) & (position < own_live * BLOCK)
    counts = jnp.sum(member.astype(jnp.float32), axis=1, keepdims=True)
    sums = cohort_sums(member.astype(jnp.bfloat16), dosage)
    extra = [jnp.broadcast_to(counts, (2 * COHORTS, TABLE))]
    if early:
        row = lax.broadcasted_iota(jnp.int32, (2 * COHORTS, early), 0)
        slot_codes = jnp.where(row == samp, cohort[None, :early].astype(jnp.float32), 0.0)
        extra.append(jnp.pad(slot_codes, ((0, 0), (0, TABLE - early))))
    sums = jnp.concatenate([sums, *extra], 1)
    surplus = swapped(coded[kept:], bits[0])
    for bit in bits[1:]:
        sums = sums + swapped(sums, bit)
    sums = sums + swapped(after(sums, surplus), bits[0])
    below, above = [dosage[:early]], [dosage[:early]]
    if early:
        for _ in range(n_var - 1):
            below.append(along_var(below[-1], 1))
            above.append(along_var(above[-1], -1))

    sum_one, sum_two = sums[:COHORTS, :width], sums[COHORTS:, :width]
    cohort_size = sums[:COHORTS, width]
    cohort_mean = sum_one / cohort_size[:, None]
    cohort_var = sum_two / cohort_size[:, None] - cohort_mean * cohort_mean
    inv_spread = lax.rsqrt(cohort_var + EPSILON)
    counts_float = weight_counts.astype(jnp.float32)
    cohort_share = counts_float / jnp.sum(counts_float)
    multiplier = inv_spread * jnp.sqrt(cohort_share / cohort_size)[:, None]
    tables = [split_parts(cohort_mean), split_parts(multiplier)]

    offset = own_live * BLOCK
    placed = lax.dynamic_update_slice_in_dim(jnp.zeros_like(coded), surplus, offset, 0)
    row_index = lax.broadcasted_iota(jnp.int32, (kept, 1), 0)
    balanced = jnp.where(row_index < offset, coded[:kept], placed[:kept])
    if early:
        balanced = after(balanced, below[2], above[2])
    if not early:
        pieces = {0: standardized(balanced, tables)}
        for bit in bits:
            pieces |= {m ^ bit: swapped(block, bit) for m, block in pieces.items()}
        groups = []
        for m in range(0, n_samp, 2):
            cols = [(pieces[i], 0, kept) for i in (m, m + 1)]
            rows = along_line(jnp.concatenate([row_part(p, 0, kept) for p, _, _ in cols], 0))
            if n_var > 4:
                rows = [rows[0], sum(rows[2:], rows[1])]
            groups.append((cols, [rows]))
        return gram_of(groups, role, 3)

    def of_panel(panel):
        chosen = jnp.zeros_like(below[0])
        for h in range(1, n_var):
            chosen += jnp.where(panel == var - h, below[h], jnp.zeros_like(below[h]))
            chosen += jnp.where(panel == var + h, above[h], jnp.zeros_like(above[h]))
        return chosen

    chip = samp // 2
    far, near, both = 4, 2, 6
    size, used = kept - early, PARTS * COHORTS
    rest = lambda m: pieces[m][early:]
    panel = lambda got: jnp.where(owns_rows, got[0], sum(got[2:], got[1]))
    other_half = lambda block: lax.dynamic_slice_in_dim(block, height - row_start, height, 1)
    my_half = lambda block: row_part(block, 0, block.shape[0])

    sent_tables = jnp.concatenate([t[:used] for t in tables], 0)
    base, first = standardized(balanced, tables, sent_tables, early)
    pieces = {0: base}
    pieces[far], pieces[near] = swapped(base, far), swapped(base, near)
    legs = [along_line(first)]
    pieces[1] = swapped(base, 1)
    legs.append(along_line(after(rest(near), pieces[1], below[3], above[3], legs[0][1], pieces[far])))
    pieces[both] = swapped(after(pieces[far], pieces[near], legs[0][1]), near)
    legs.append(along_line(after(rest(far), legs[0][1])))
    up = jnp.concatenate([of_panel(chip ^ 2), of_panel(chip ^ 3)], 0)
    up = swapped(after(up, legs[1][1]), far)
    pieces[both + 1] = swapped(after(pieces[both], *legs[0][2:], legs[1][1]), 1)
    done = (legs[2][1], *legs[1][2:])
    tail = [row_part(pieces[m], early, size) for m in (both, both + 1)]
    legs.append(along_line(after(tail[0], legs[2][1]), *legs[2][2:]))
    legs.append(along_line(after(tail[1], *done), *legs[2][2:], *legs[3][2:]))
    aside = jnp.concatenate([of_panel(chip ^ 1), up[early:]], 0)
    aside = swapped(after(aside, *done), near)
    brought = jnp.concatenate([of_panel(chip), aside[:early], up[:early], aside[early:]], 0)
    other = swapped(brought, 1)
    pieces[far + 1] = swapped(after(pieces[far], pieces[both + 1]), 1)
    pieces[near + 1] = swapped(after(pieces[near], pieces[far + 1]), 1)
    whole = [panel([part[:size] for part in leg]) for leg in legs[:3]]
    others = [swapped(other_half(block), 1) for block in whole]

    row_tables = my_half(panel([part[size:] for part in legs[0]]))
    pad = jnp.zeros((TABLE - used, height), jnp.bfloat16)
    row_tables = [jnp.concatenate([row_tables[i : i + used], pad], 0) for i in (0, used)]
    order = [*range(0, n_samp, 2), *range(1, n_samp, 2)]
    source = samp ^ jnp.asarray(order, jnp.int32)
    pick = (source[:, None] == jnp.arange(n_samp)[None, :]).astype(jnp.float32)
    early_codes = jnp.dot(pick, sums[:n_samp, width + TABLE : width + TABLE + early])
    lanes = jnp.broadcast_to(early_codes.reshape(-1, 1), (n_samp * early, TABLE))
    brought = jnp.concatenate([my_half(brought), my_half(other)], 0)
    brought = standardized(jnp.concatenate([brought, lanes.astype(jnp.bfloat16)], 1), row_tables)
    own = jnp.concatenate([row_part(pieces[m], 0, early) for m in order], 0)

    cols = lambda *ms: [(pieces[m], early, size) for m in ms]
    groups = [([(pieces[m], 0, early) for m in order], [[own, brought]])]
    groups += [
        (cols(i, i + 1), [[my_half(block)], [other]])
        for i, block, other in zip((0, near, far), whole, others)
    ]
    groups.append((cols(both, both + 1), legs[3:]))
    return gram_of(groups, role, 4)


def solution(mesh):
    placed = (P("samp", "var"), P("samp"), P("samp"), P())
    return jax.shard_map(
        shards, mesh=mesh, in_specs=placed, out_specs=P("samp", "var"), check_vma=False
    )
```
